256 devices in a mesh: grp: 4 (over z_hi, core), fsdp: 64 (over x, z_lo, y).
Axes of the slice: x: 4, y: 4, z: 8 (z_hi: 2, z_lo: 4; z = z_hi * 4 + z_lo), core: 2. Of those that a mesh axis runs over, the one named last changes fastest.
Arguments:
- acts: bfloat16 [4, 65536, 4096], P('grp', 'fsdp'), may hold values from -16 to 16
- cotangent: bfloat16 [4, 65536, 1024], P('grp', 'fsdp'), may hold values from -0.0234375 to 0.0234375
- inner_weights: float32 [4, 4096, 1024], P('grp', 'fsdp'), may hold values from -6 to 6
- first_moment: float32 [4, 4096, 1024], P('grp', 'fsdp'), may hold values from -0.6 to 0.6
- second_moment: float32 [4, 4096, 1024], P('grp', 'fsdp'), may hold values from 0.01 to 0.1
- outer_weights: float32 [4096, 1024], P('fsdp'), may hold values from -6 to 6
- outer_momentum: float32 [4096, 1024], P('fsdp'), may hold values from -3 to 3
- writer_of: int32 [64, 64], P('fsdp'), may hold values from 0 to 3, as said below
Outputs:
- outer_next: float32 [64, 64, 1024], P('fsdp', 'grp')
- momentum_next: float32 [64, 64, 1024], P('fsdp', 'grp')
- written: float32 [64, 128, 2048], P('fsdp', 'grp')
The draws below stay inside these ranges and needn't reach their ends.
Inputs may be any that keep to these rules, and one draw needn't show every extreme that they name: In each block of 16 consecutive entries of a row of writer_of, no value occurs more than 8 times, and in every row one value occurs exactly 8 times in each of its blocks.
All inputs are finite; a program needn't handle non-finite values.
Results may differ from the reference program's by a relative error of at most 0.0003.
Values sent between devices are 32-bit elements; how exact they have to be, the bound alone decides.
No kernel may reach another device: no remote copies, remote signals or barrier semaphores. Data moves between devices by JAX's collectives and lax.ppermute only.
A program may use at most 128 MiB of HBM per device.

```python
import math
import jax
import jax.numpy as jnp
from jax import lax

ROWS = 4096
COLS = 1024
TOK_DEV = 1024
INNER_STEP = 100
TOK_GRP = 65536
SHARE = 16
PAIR = 8
N_GRP = 4
N_FSDP = 64


def draw_writer_of(key, part):
    key = jax.random.fold_in(key, 7)
    heavy_key, other_key, order_key = jax.random.split(key, 3)
    heavy = jax.random.randint(heavy_key, (N_FSDP, 1, 1), 0, N_GRP)
    offsets = jax.random.randint(other_key, (N_FSDP, N_GRP, SHARE - PAIR), 1, N_GRP)
    others = (heavy + offsets) % N_GRP
    base = jnp.concatenate([jnp.broadcast_to(heavy, (N_FSDP, N_GRP, PAIR)), others], axis=2)
    scores = jax.random.randint(order_key, (N_FSDP, N_GRP, SHARE), 0, 1048576) * SHARE + jnp.arange(SHARE, dtype=jnp.int32)
    order = jnp.argsort(scores, axis=2, stable=True)
    mixed = jnp.take_along_axis(base, order, axis=2)
    return mixed.reshape(N_FSDP, N_GRP * SHARE).astype(jnp.int32)


def strengthened(values, own_key, source, target, shards_of, factor):
    def block_of(position):
        return (jnp.arange(values.shape[position]) // (values.shape[position] // shards_of)).reshape((-1,) + (1,) * (values.ndim - 1 - position))

    first = jax.random.permutation(own_key, shards_of)[block_of(target)]
    other_side = (block_of(target) + shards_of // 2) % shards_of
    return jnp.where((block_of(source) == first) | (block_of(source) == other_side), factor * values, values)


def level_of(stream_key, dims, shards, smallest, largest):
    def one(position, shards_of):
        draws = jax.random.uniform(jax.random.fold_in(jax.random.fold_in(stream_key, 6), position), (shards_of,), jnp.float32, smallest / len(shards), largest / len(shards))
        return jnp.repeat(jnp.exp(draws), dims[position] // shards_of).reshape((-1,) + (1,) * (len(dims) - position - 1))

    gain = one(*shards[0])
    for cut in shards[1:]:
        gain = gain * one(*cut)
    return gain


def gaussian(own_key, shape, scale, limit, shards=(), kind=jnp.bfloat16):
    factor_of = level_of(own_key, shape, shards, -0.22, 0.18) if shards else 1.0
    values = jax.random.normal(own_key, shape, jnp.float32) * scale * factor_of
    return jnp.minimum(jnp.maximum(values, -limit), limit).astype(kind)


def noise_with(key, dims, spread, limit, cuts, heavy, held_as=jnp.bfloat16):
    array = spread * jax.random.normal(key, dims, jnp.float32)
    if cuts:
        array = array * level_of(key, dims, cuts, -0.22, 0.18)
    return jnp.clip(strengthened(array, jax.random.fold_in(key, 3), *heavy), -limit, limit).astype(held_as)


def setup_inputs(seed: int = 0) -> dict:
    streams_of = jax.random.split(jax.random.key(seed), 9)
    return {
        "acts": noise_with(streams_of[0], (N_GRP, TOK_GRP, ROWS), 1.0, 16.0, ((0, 4), (1, 64)), (1, 2, 64, 4.0)),
        "cotangent": gaussian(streams_of[1], (N_GRP, TOK_GRP, COLS), (TOK_DEV * N_FSDP) ** -0.5, 0.0234375, ((0, 4), (1, 64))),
        "inner_weights": gaussian(streams_of[2], (N_GRP, ROWS, COLS), 1.0, 6.0, ((0, 4), (1, 64)), jnp.float32),
        "first_moment": gaussian(streams_of[3], (N_GRP, ROWS, COLS), 0.1, 0.6, ((0, 4), (1, 64)), jnp.float32),
        "second_moment": jnp.clip(jnp.exp(math.log(0.1) - 2.3025851 * jax.random.uniform(streams_of[4], (N_GRP, ROWS, COLS), jnp.float32) ** level_of(streams_of[4], (N_GRP, ROWS, COLS), ((0, 4), (1, 64)), -0.2, 0.2)), 0.01, 0.1),
        "outer_weights": gaussian(streams_of[5], (ROWS, COLS), 1.0, 6.0, ((0, 64),), jnp.float32),
        "outer_momentum": gaussian(streams_of[6], (ROWS, COLS), 0.5, 3.0, ((0, 64),), jnp.float32),
        "writer_of": draw_writer_of(jax.random.fold_in(streams_of[8], 71), 0),
    }


BETA_ONE = 0.9
BETA_TWO = 0.95
INNER_RATE = 0.4
DECAY_RATE = 0.1
EPSILON = 1e-08
OUTER_RATE = 0.8
MOMENTUM = 0.9

def adam_update(weights, first_mom, second, gradient):
    first_new = BETA_ONE * first_mom + (1.0 - BETA_ONE) * gradient
    second_new = BETA_TWO * second + (1.0 - BETA_TWO) * gradient * gradient
    first_hat = first_new / (1.0 - BETA_ONE ** INNER_STEP)
    second_hat = second_new / (1.0 - BETA_TWO ** INNER_STEP)
    return weights - INNER_RATE * (first_hat / (jnp.sqrt(second_hat) + EPSILON) + DECAY_RATE * weights)

def slot_ranks(writer_ids, group_count):
    onehot = (writer_ids[..., None] == jnp.arange(group_count, dtype=jnp.int32)).astype(jnp.int32)
    before = jnp.cumsum(onehot, axis=-2) - onehot
    return lax.optimization_barrier(jnp.sum(before * onehot, axis=-1))

def reference(acts, cotangent, inner_weights, first_moment, second_moment, outer_weights, outer_momentum, writer_of):
    summed_steps = jnp.zeros((ROWS, COLS), jnp.float32)
    for group_index in range(N_GRP):
        gradient = jnp.dot(acts[group_index].T, cotangent[group_index], preferred_element_type=jnp.float32)
        summed_steps = summed_steps + adam_update(inner_weights[group_index], first_moment[group_index], second_moment[group_index], gradient)
    pseudo_grad = outer_weights - summed_steps / N_GRP
    momentum_next = MOMENTUM * outer_momentum + pseudo_grad
    outer_next = outer_weights - OUTER_RATE * (pseudo_grad + MOMENTUM * momentum_next)
    packed = jnp.concatenate([outer_next, momentum_next], axis=1)
    writer_ids = writer_of.reshape(N_FSDP, N_GRP, SHARE).astype(jnp.int32)
    slot_rank = slot_ranks(writer_ids, N_GRP)
    sender = jnp.arange(N_GRP, dtype=jnp.int32)[None, :, None]
    target = writer_ids * (N_GRP * PAIR) + sender * PAIR + slot_rank
    shard_index = jnp.broadcast_to(jnp.arange(N_FSDP, dtype=jnp.int32)[:, None, None], writer_ids.shape)
    written = jnp.zeros((N_FSDP, N_GRP * N_GRP * PAIR, 2 * COLS), jnp.float32)
    written = written.at[shard_index.reshape(-1), target.reshape(-1)].set(packed)
    out_shape = (N_FSDP, ROWS // N_FSDP, COLS)
    return (outer_next.reshape(out_shape), momentum_next.reshape(out_shape), written)
```

```python
import functools

import jax
import jax.numpy as jnp
from jax import lax
from jax.experimental import pallas as pl
from jax.experimental.pallas import tpu as pltpu
from jax.sharding import Mesh, PartitionSpec as P

INNER_STEP = 100
BETA_ONE = 0.9
BETA_TWO = 0.95
INNER_RATE = 0.4
DECAY_RATE = 0.1
EPSILON = 1e-08
OUTER_RATE = 0.8
MOMENTUM = 0.9

GRP = ("zh", "core")
FSDP = ("x", "z", "y")
CHUNKS = (
    ("a", 0, 256, 0),
    ("b", 256, 256, 0),
    ("a", 512, 256, 1),
    ("b", 768, 256, 1),
)


def adam_update(weights, first_mom, second, gradient):
    first_new = BETA_ONE * first_mom + (1.0 - BETA_ONE) * gradient
    second_new = BETA_TWO * second + (1.0 - BETA_TWO) * gradient * gradient
    first_hat = first_new / (1.0 - BETA_ONE**INNER_STEP)
    second_hat = second_new / (1.0 - BETA_TWO**INNER_STEP)
    return weights - INNER_RATE * (
        first_hat / (jnp.sqrt(second_hat) + EPSILON) + DECAY_RATE * weights
    )


def slot_ranks(writer_ids, group_count):
    onehot = (writer_ids[..., None] == jnp.arange(group_count, dtype=jnp.int32)).astype(jnp.int32)
    before = jnp.cumsum(onehot, axis=-2) - onehot
    return jnp.sum(before * onehot, axis=-1)


def ring_partners(p, flip):
    near, far = p ^ 1, 3 - p
    return (far, near) if flip else (near, far)


def ring_order(p, flip):
    near, far = p ^ 1, 3 - p
    first = jnp.where(flip, far, near)
    second = jnp.where(flip, near, far)
    return [p ^ 2, first, second, p]


def line_order(p):
    return [3 - p, p ^ 1, p ^ 2, p]


def ring_permute(value, axis, variant, step):
    perm = []
    for core in range(2):
        for p in range(4):
            q = ring_partners(p, (core + variant) % 2)[step]
            perm.append((core * 4 + p, core * 4 + q))
    return lax.ppermute(value, ("core", axis), perm)


def line_permute(value, step):
    bit = 1 + step
    return lax.ppermute(value, "z", [(p, p ^ bit) for p in range(4)])


def halve(send, keep, permute):
    got = permute(send, 0)
    passed = keep[0] + got[0]
    got_two = permute(passed, 1)
    return keep[1] + got[1] + got_two


def product_kernel(order, acts, cot, *rest, kind):
    outs, result = rest[:-1], rest[-1]
    result[...] = lax.dot_general(
        acts[...], cot[...], (((0,), (0,)), ((), ())), preferred_element_type=jnp.float32
    )
    for rank in range(4):
        rows = result[pl.ds(pl.multiple_of(order[4 + rank] * 64, 64), 64), :]
        if kind == "a":
            outs[0][0, rank, 0] = rows
        else:
            outs[rank // 2][rank % 2, 0, 0] = rows


def products(order, acts, cot, kind, col, width, first, count):
    tokens = acts.shape[0]
    if kind == "a":
        out_shape = [jax.ShapeDtypeStruct((count, 4, 4, 64, width), jnp.float32)]
        out_specs = [pl.BlockSpec((1, 4, 1, 64, width), lambda i, j, o: (i, 0, j, 0, 0))]
    else:
        out_shape = [jax.ShapeDtypeStruct((2, 4, 4, 64, width), jnp.float32)] * 2
        out_specs = [pl.BlockSpec((2, 1, 1, 64, width), lambda i, j, o: (0, i, j, 0, 0))] * 2
    return pl.pallas_call(
        functools.partial(product_kernel, kind=kind),
        out_shape=out_shape,
        grid_spec=pltpu.PrefetchScalarGridSpec(
            num_scalar_prefetch=1,
            grid=(count, 4),
            in_specs=[
                pl.BlockSpec((tokens, 256), lambda i, j, o: (0, o[first + i] * 4 + o[8 + j])),
                pl.BlockSpec((tokens, width), lambda i, j, o: (0, col // width)),
            ],
            out_specs=out_specs,
            scratch_shapes=[pltpu.VMEM((256, width), jnp.float32)],
        ),
        cost_estimate=pl.CostEstimate(
            flops=2 * tokens * count * 1024 * width,
            bytes_accessed=2 * tokens * count * 1024 + 4 * count * 1024 * width,
            transcendentals=0,
        ),
        name="products_" + kind,
    )(order, acts, cot)


def body(
    acts,
    cotangent,
    inner_weights,
    first_moment,
    second_moment,
    outer_weights,
    outer_momentum,
    writer_of,
):
    tokens = acts[0]
    upstream = cotangent[0]
    core = lax.axis_index("core")
    spot = {axis: lax.axis_index(axis) for axis in FSDP}

    pieces = []
    for kind, col, width, variant in CHUNKS:
        flip = (core + variant) % 2 == 1
        order = jnp.stack(
            ring_order(spot["x"], flip) + ring_order(spot["y"], flip) + line_order(spot["z"])
        ).astype(jnp.int32)
        if kind == "a":
            (send,) = products(order, tokens, upstream, kind, col, width, 0, 2)
            (keep,) = products(order, tokens, upstream, kind, col, width, 2, 2)
        else:
            send, keep = products(order, tokens, upstream, kind, col, width, 0, 4)
        axes = ("x", "y") if kind == "a" else ("y", "x")
        part = halve(send, keep, lambda v, s: ring_permute(v, axes[0], variant, s))
        part = halve(part[:2], part[2:], lambda v, s: ring_permute(v, axes[1], variant, s))
        part = halve(part[:2], part[2:], line_permute)
        cols = slice(col, col + width)
        pieces.append(
            adam_update(
                inner_weights[0][:, cols],
                first_moment[0][:, cols],
                second_moment[0][:, cols],
                part,
            )
        )
    stepped = jnp.concatenate(pieces, axis=1)

    swap = [(0, 1), (1, 0)]
    halves = stepped.reshape(2, 32, stepped.shape[1])
    mine = lax.dynamic_index_in_dim(halves, core, 0, keepdims=False)
    other = lax.dynamic_index_in_dim(halves, 1 - core, 0, keepdims=False)
    pair = mine + lax.ppermute(other, "core", swap)
    total = pair + lax.ppermute(pair, "zh", swap)
    total_other = lax.ppermute(total, "core", swap)
    low = jnp.where(core == 0, total, total_other)
    high = jnp.where(core == 0, total_other, total)
    group_sum = jnp.concatenate([low, high], axis=0)

    group_count = 4
    group_index = lax.axis_index(GRP)
    share_rows = 16
    pair_slots = 8
    pseudo_grad = outer_weights - group_sum / group_count
    momentum_new = MOMENTUM * outer_momentum + pseudo_grad
    outer_new = outer_weights - OUTER_RATE * (pseudo_grad + MOMENTUM * momentum_new)

    writers = writer_of.reshape(group_count, share_rows)
    ranks = slot_ranks(writers, group_count)
    sender = jnp.arange(group_count, dtype=jnp.int32)[:, None]
    target = jnp.where(writers == group_index, sender * pair_slots + ranks, -1).reshape(-1)
    slots = jnp.arange(group_count * pair_slots, dtype=jnp.int32)
    placing = (target[None, :] == slots[:, None]).astype(jnp.float32)
    packed = jnp.concatenate([outer_new, momentum_new], axis=1)
    written = jnp.einsum("pr,rc->pc", placing, packed, precision=lax.Precision.HIGHEST)

    def own(rows):
        return lax.dynamic_slice_in_dim(rows, group_index * share_rows, share_rows, 0)[None]

    return own(outer_new), own(momentum_new), written[None]


def solution(mesh):
    fine = Mesh(mesh.devices.reshape(2, 2, 4, 4, 4), GRP + FSDP)
    return jax.shard_map(
        body,
        mesh=fine,
        in_specs=(
            P(GRP, FSDP, None),
            P(GRP, FSDP, None),
            P(GRP, FSDP, None),
            P(GRP, FSDP, None),
            P(GRP, FSDP, None),
            P(FSDP, None),
            P(FSDP, None),
            P(FSDP, None),
        ),
        out_specs=(P(FSDP, GRP, None), P(FSDP, GRP, None), P(FSDP, GRP, None)),
        check_vma=False,
    )
```

```python
import functools

import jax
import jax.numpy as jnp
from jax import lax
from jax.experimental import pallas as pl
from jax.experimental.pallas import tpu as pltpu
from jax.sharding import Mesh, PartitionSpec as P

INNER_STEP = 100
BETA_ONE = 0.9
BETA_TWO = 0.95
INNER_RATE = 0.4
DECAY_RATE = 0.1
EPSILON = 1e-08
OUTER_RATE = 0.8
MOMENTUM = 0.9

GRP = ("zh", "core")
FSDP = ("x", "z", "y")
SIDE = 8
MAIN = 64 - SIDE
HALF = 512


def adam_update(weights, first_mom, second, gradient):
    first_new = BETA_ONE * first_mom + (1.0 - BETA_ONE) * gradient
    second_new = BETA_TWO * second + (1.0 - BETA_TWO) * gradient * gradient
    first_hat = first_new / (1.0 - BETA_ONE**INNER_STEP)
    second_hat = second_new / (1.0 - BETA_TWO**INNER_STEP)
    return weights - INNER_RATE * (
        first_hat / (jnp.sqrt(second_hat) + EPSILON) + DECAY_RATE * weights
    )


def slot_ranks(writer_ids, group_count):
    onehot = (writer_ids[..., None] == jnp.arange(group_count, dtype=jnp.int32)).astype(jnp.int32)
    before = jnp.cumsum(onehot, axis=-2) - onehot
    return jnp.sum(before * onehot, axis=-1)


def ring_partners(p, flip):
    near, far = p ^ 1, 3 - p
    return (far, near) if flip else (near, far)


def ring_order(p, flip):
    near, far = p ^ 1, 3 - p
    first = jnp.where(flip, far, near)
    second = jnp.where(flip, near, far)
    return [p ^ 2, first, second, p]


def ring_permute(value, axis, variant, step):
    perm = []
    for core in range(2):
        for p in range(4):
            q = ring_partners(p, (core + variant) % 2)[step]
            perm.append((core * 4 + p, core * 4 + q))
    return lax.ppermute(value, ("core", axis), perm)


def line_permute(value, step):
    bit = 1 + step
    return lax.ppermute(value, "z", [(p, p ^ bit) for p in range(4)])


def behind(value, earlier):
    return lax.optimization_barrier((value, earlier))[0]


X_ORDER, Y_ORDER, Y_FLIPPED, LOW_BIT, HIGH_BIT = 0, 4, 8, 12, 13


def product_rows(place, acts, cot, result, low):
    result[...] = lax.dot_general(
        acts[...], cot[...], (((0,), (0,)), ((), ())), preferred_element_type=jnp.float32
    )

    def rows(z, y, start, count, cols):
        offset = pl.multiple_of(z * 256 + y * 64 + start, 8)
        return result[pl.ds(offset, count), cols]

    return rows


FIRST, SECOND = slice(0, HALF), slice(HALF, 2 * HALF)


def sides(place, side, rows):
    for z in range(2):
        low = jnp.where(place[LOW_BIT] == z, 1, 0)
        for y in range(4):
            side[low, 0, 0, y] = rows(z, place[Y_ORDER + y], MAIN, SIDE, slice(0, 2 * HALF))


def early_kernel(place, acts, cot, a_send, c_send, c_keep, b_send, b_keep, side, result):
    rows = product_rows(place, acts, cot, result, None)
    sides(place, side, rows)
    step = pl.program_id(0)
    for z in range(2):
        low = jnp.where(place[LOW_BIT] == z, 1, 0)
        for y in range(2):
            a_send[0, y, low, 0] = rows(z, place[Y_ORDER + y], 0, MAIN, FIRST)
            b_send[y, 0, low, 0] = rows(z, place[Y_ORDER + y], 0, MAIN, SECOND)
            b_keep[y, 0, low, 0] = rows(z, place[Y_ORDER + 2 + y], 0, MAIN, SECOND)

    @pl.when(step == 0)
    def _():
        for z in range(2):
            low = jnp.where(place[LOW_BIT] == z, 1, 0)
            for y in range(2):
                c_send[0, y, low, 0] = rows(z, place[Y_ORDER + 2 + y], 0, MAIN, FIRST)

    @pl.when(step == 1)
    def _():
        for z in range(2):
            low = jnp.where(place[LOW_BIT] == z, 1, 0)
            for y in range(2):
                c_keep[0, y, low, 0] = rows(z, place[Y_ORDER + 2 + y], 0, MAIN, FIRST)


def late_kernel(
    place, acts, cot, c_send_in, c_keep_in, side_in, a_keep, c_send, c_keep, b_send, b_keep, side, result
):
    rows = product_rows(place, acts, cot, result, None)
    sides(place, side, rows)
    step = pl.program_id(0)
    for z in range(2):
        low = jnp.where(place[LOW_BIT] == z, 1, 0)
        for y in range(2):
            a_keep[0, y, low, 0] = rows(z, place[Y_ORDER + y], 0, MAIN, FIRST)
            b_send[y, 0, low, 0] = rows(z, place[Y_FLIPPED + y], 0, MAIN, SECOND)
            b_keep[y, 0, low, 0] = rows(z, place[Y_FLIPPED + 2 + y], 0, MAIN, SECOND)

    @pl.when(step == 0)
    def _():
        for z in range(2):
            low = jnp.where(place[LOW_BIT] == z, 1, 0)
            for y in range(2):
                c_send[0, y, low, 0] = rows(z, place[Y_ORDER + 2 + y], 0, MAIN, FIRST)

    @pl.when(step == 1)
    def _():
        for z in range(2):
            low = jnp.where(place[LOW_BIT] == z, 1, 0)
            for y in range(2):
                c_keep[0, y, low, 0] = rows(z, place[Y_ORDER + 2 + y], 0, MAIN, FIRST)


def products(place, acts, cot, earlier):
    tokens = acts.shape[0]
    late = earlier is not None
    first = 2 if late else 0
    part = (2, 2, 2, 2, MAIN, HALF)
    piece = jax.ShapeDtypeStruct(part, jnp.float32)
    block = (1, 2, 2, 1, MAIN, HALF)
    by_x = pl.BlockSpec(block, lambda i, j, o: (i, 0, 0, o[HIGH_BIT] ^ j ^ 1, 0, 0))
    by_y = pl.BlockSpec(
        (2, 1, 2, 1, MAIN, HALF), lambda i, j, o: (0, i, 0, o[HIGH_BIT] ^ j ^ 1, 0, 0)
    )
    slot = 1 if late else 0
    at_first = pl.BlockSpec(
        block,
        lambda i, j, o: (slot, 0, 0, jnp.where(i == 0, o[HIGH_BIT] ^ j ^ 1, o[HIGH_BIT]), 0, 0),
    )
    at_second = pl.BlockSpec(
        block,
        lambda i, j, o: (slot, 0, 0, jnp.where(i == 0, o[HIGH_BIT] ^ 1, o[HIGH_BIT] ^ j ^ 1), 0, 0),
    )
    side_shape = jax.ShapeDtypeStruct((2, 2, 4, 4, SIDE, 2 * HALF), jnp.float32)
    side = pl.BlockSpec(
        (2, 1, 1, 4, SIDE, 2 * HALF),
        lambda i, j, o: (0, o[HIGH_BIT] ^ j ^ 1, first + i, 0, 0, 0),
    )
    any_spec = pl.BlockSpec(memory_space=pl.ANY)
    return pl.pallas_call(
        late_kernel if late else early_kernel,
        out_shape=[piece] * 5 + [side_shape],
        grid_spec=pltpu.PrefetchScalarGridSpec(
            num_scalar_prefetch=1,
            grid=(2, 2),
            in_specs=[
                pl.BlockSpec((tokens, 512), lambda i, j, o: (0, o[X_ORDER + first + i] * 2 + j)),
                pl.BlockSpec((tokens, 2 * HALF), lambda i, j, o: (0, 0)),
            ]
            + [any_spec] * (3 if late else 0),
            out_specs=[by_x, at_first, at_second, by_y, by_y, side],
            scratch_shapes=[pltpu.VMEM((512, 2 * HALF), jnp.float32)],
        ),
        input_output_aliases={3: 1, 4: 2, 5: 5} if late else {},
        compiler_params=pltpu.CompilerParams(vmem_limit_bytes=60 * 2**20),
        cost_estimate=pl.CostEstimate(
            flops=2 * tokens * 2048 * 1024 * (1 if late else 1),
            bytes_accessed=2 * tokens * 3072 + 4 * 2048 * 1024,
            transcendentals=0,
        ),
        name="products_late" if late else "products_early",
    )(place, acts, cot, *(earlier or ()))


def body(
    acts,
    cotangent,
    inner_weights,
    first_moment,
    second_moment,
    outer_weights,
    outer_momentum,
    writer_of,
):
    tokens = acts[0]
    upstream = cotangent[0]
    core = lax.axis_index("core")
    spot = {axis: lax.axis_index(axis) for axis in FSDP}

    flip = core == 1
    place = jnp.stack(
        ring_order(spot["x"], flip)
        + ring_order(spot["y"], flip)
        + ring_order(spot["y"], ~flip)
        + [spot["z"] & 1, spot["z"] >> 1]
    ).astype(jnp.int32)
    a_send, c_send, c_keep, b_send, b_keep, side = products(place, tokens, upstream, None)
    a_keep, c_send, c_keep, d_send, d_keep, side = products(
        place, tokens, upstream, (c_send, c_keep, side)
    )

    def along(axis, variant):
        return lambda value, step: ring_permute(value, axis, variant, step)

    last = []

    def turn(value):
        if last:
            value = behind(value, last[-1])
        last.append(value)
        return value

    x_one, y_one, x_two, y_two = along("x", 0), along("y", 0), along("x", 1), along("y", 1)
    a_got = x_one(a_send, 0)
    b_got = y_one(b_send, 0)
    c_got = x_two(c_send, 0)
    d_got = y_two(d_send, 0)
    s_got = line_permute(turn(side[0]), 0)
    group_count = 4
    group_index = lax.axis_index(GRP)
    share_rows = 16
    pair_slots = 8
    writers = writer_of.reshape(group_count, share_rows)
    ranks = slot_ranks(writers, group_count)
    sender = jnp.arange(group_count, dtype=jnp.int32)[:, None]
    target = jnp.where(writers == group_index, sender * pair_slots + ranks, -1).reshape(-1)
    slots = jnp.arange(group_count * pair_slots, dtype=jnp.int32)
    placing = turn((target[None, :] == slots[:, None]).astype(jnp.float32))
    a_more = x_one(turn(a_keep[0] + a_got[0]), 1)
    b_more = y_one(turn(b_keep[0] + b_got[0]), 1)
    c_more = x_two(turn(c_keep[0] + c_got[0]), 1)
    d_more = y_two(turn(d_keep[0] + d_got[0]), 1)
    s_more = line_permute(turn(side[1, 0] + s_got[0]), 1)
    a_in = y_one(turn(a_keep[1] + a_got[1] + a_more), 0)
    b_in = x_one(turn(b_keep[1] + b_got[1] + b_more), 0)
    c_sum = c_keep[1] + c_got[1] + c_more
    d_sum = d_keep[1] + d_got[1] + d_more
    side = side[1, 1] + s_got[1] + s_more
    s_got = x_one(turn(side[:2]), 0)
    a_last = y_one(turn(c_sum[0] + a_in[0]), 1)
    b_last = x_one(turn(d_sum[0] + b_in[0]), 1)
    parts = jnp.concatenate([c_sum[1] + a_in[1] + a_last, d_sum[1] + b_in[1] + b_last], axis=-1)
    s_more = x_one(turn(side[2] + s_got[0]), 1)
    z_got = line_permute(turn(parts[0]), 0)
    side = side[3] + s_got[1] + s_more
    s_got = y_one(turn(side[:2]), 0)
    s_more = y_one(turn(side[2] + s_got[0]), 1)
    z_more = line_permute(turn(parts[1, 0] + z_got[0]), 1)
    side = side[3] + s_got[1] + s_more
    main_rows = parts[1, 1] + z_got[1] + z_more
    gradient = jnp.concatenate([main_rows, side], axis=0)
    stepped = adam_update(inner_weights[0], first_moment[0], second_moment[0], gradient)

    swap = [(0, 1), (1, 0)]
    halves = stepped.reshape(2, 32, stepped.shape[1])
    mine = lax.dynamic_index_in_dim(halves, core, 0, keepdims=False)
    other = lax.dynamic_index_in_dim(halves, 1 - core, 0, keepdims=False)
    pair = mine + lax.ppermute(other, "core", swap)
    total = pair + lax.ppermute(pair, "zh", swap)
    total_other = lax.ppermute(total, "core", swap)
    low = jnp.where(core == 0, total, total_other)
    high = jnp.where(core == 0, total_other, total)
    group_sum = jnp.concatenate([low, high], axis=0)

    pseudo_grad = outer_weights - group_sum / group_count
    momentum_new = MOMENTUM * outer_momentum + pseudo_grad
    outer_new = outer_weights - OUTER_RATE * (pseudo_grad + MOMENTUM * momentum_new)

    packed = jnp.concatenate([outer_new, momentum_new], axis=1)
    written = jnp.einsum("pr,rc->pc", placing, packed, precision=lax.Precision.HIGHEST)

    def own(rows):
        return lax.dynamic_slice_in_dim(rows, group_index * share_rows, share_rows, 0)[None]

    return own(outer_new), own(momentum_new), written[None]


def solution(mesh):
    fine = Mesh(mesh.devices.reshape(2, 2, 4, 4, 4), GRP + FSDP)
    return jax.shard_map(
        body,
        mesh=fine,
        in_specs=(
            P(GRP, FSDP, None),
            P(GRP, FSDP, None),
            P(GRP, FSDP, None),
            P(GRP, FSDP, None),
            P(GRP, FSDP, None),
            P(FSDP, None),
            P(FSDP, None),
            P(FSDP, None),
        ),
        out_specs=(P(FSDP, GRP, None), P(FSDP, GRP, None), P(FSDP, GRP, None)),
        check_vma=False,
    )
```

```python
import functools

import jax
import jax.numpy as jnp
from jax import lax
from jax.experimental import pallas as pl
from jax.experimental.pallas import tpu as pltpu
from jax.sharding import Mesh, PartitionSpec as P

INNER_STEP = 100
BETA_ONE = 0.9
BETA_TWO = 0.95
INNER_RATE = 0.4
DECAY_RATE = 0.1
EPSILON = 1e-08
OUTER_RATE = 0.8
MOMENTUM = 0.9

GRP = ("zh", "core")
FSDP = ("x", "z", "y")
SIDE = 8
MAIN = 64 - SIDE
HALF = 512


def adam_update(weights, first_mom, second, gradient):
    first_new = BETA_ONE * first_mom + (1.0 - BETA_ONE) * gradient
    second_new = BETA_TWO * second + (1.0 - BETA_TWO) * gradient * gradient
    first_hat = first_new / (1.0 - BETA_ONE**INNER_STEP)
    second_hat = second_new / (1.0 - BETA_TWO**INNER_STEP)
    return weights - INNER_RATE * (
        first_hat / (jnp.sqrt(second_hat) + EPSILON) + DECAY_RATE * weights
    )


def ring_partners(p, flip):
    near, far = p ^ 1, 3 - p
    return (far, near) if flip else (near, far)


def ring_order(p, flip):
    near, far = p ^ 1, 3 - p
    first = jnp.where(flip, far, near)
    second = jnp.where(flip, near, far)
    return [p ^ 2, first, second, p]


def ring_permute(value, axis, variant, step):
    perm = []
    for core in range(2):
        for p in range(4):
            q = ring_partners(p, (core + variant) % 2)[step]
            perm.append((core * 4 + p, core * 4 + q))
    return lax.ppermute(value, ("core", axis), perm)


def line_permute(value, step):
    bit = 1 + step
    return lax.ppermute(value, "z", [(p, p ^ bit) for p in range(4)])


def behind(value, earlier):
    return lax.optimization_barrier((value, earlier))[0]


X_ORDER, Y_ORDER, Y_FLIPPED, LOW_BIT, HIGH_BIT = 0, 4, 8, 12, 13


def product_rows(place, acts, cot, result, low):
    result[...] = lax.dot_general(
        acts[...], cot[...], (((0,), (0,)), ((), ())), preferred_element_type=jnp.float32
    )

    def rows(z, y, start, count, cols):
        offset = pl.multiple_of(z * 256 + y * 64 + start, 8)
        return result[pl.ds(offset, count), cols]

    return rows


FIRST, SECOND = slice(0, HALF), slice(HALF, 2 * HALF)


def sides(place, side, rows):
    for z in range(2):
        low = jnp.where(place[LOW_BIT] == z, 1, 0)
        for y in range(4):
            side[low, 0, 0, y] = rows(z, place[Y_ORDER + y], MAIN, SIDE, slice(0, 2 * HALF))


def early_kernel(place, acts, cot, a_send, c_send, c_keep, b_send, b_keep, side, result):
    rows = product_rows(place, acts, cot, result, None)
    sides(place, side, rows)
    step = pl.program_id(0)
    for z in range(2):
        low = jnp.where(place[LOW_BIT] == z, 1, 0)
        for y in range(2):
            a_send[0, low, y, 0] = rows(z, place[Y_ORDER + y], 0, MAIN, FIRST)
            b_send[y, low, 0, 0] = rows(z, place[Y_ORDER + y], 0, MAIN, SECOND)
            b_keep[y, low, 0, 0] = rows(z, place[Y_ORDER + 2 + y], 0, MAIN, SECOND)

    @pl.when(step == 0)
    def _():
        for z in range(2):
            low = jnp.where(place[LOW_BIT] == z, 1, 0)
            for y in range(2):
                c_send[0, low, y, 0] = rows(z, place[Y_ORDER + 2 + y], 0, MAIN, FIRST)

    @pl.when(step == 1)
    def _():
        for z in range(2):
            low = jnp.where(place[LOW_BIT] == z, 1, 0)
            for y in range(2):
                c_keep[0, low, y, 0] = rows(z, place[Y_ORDER + 2 + y], 0, MAIN, FIRST)


def late_kernel(
    place, acts, cot, c_send_in, c_keep_in, side_in, a_keep, c_send, c_keep, b_send, b_keep, side, result
):
    rows = product_rows(place, acts, cot, result, None)
    sides(place, side, rows)
    step = pl.program_id(0)
    for z in range(2):
        low = jnp.where(place[LOW_BIT] == z, 1, 0)
        for y in range(2):
            a_keep[0, low, y, 0] = rows(z, place[Y_ORDER + y], 0, MAIN, FIRST)
            b_send[y, low, 0, 0] = rows(z, place[Y_FLIPPED + y], 0, MAIN, SECOND)
            b_keep[y, low, 0, 0] = rows(z, place[Y_FLIPPED + 2 + y], 0, MAIN, SECOND)

    @pl.when(step == 0)
    def _():
        for z in range(2):
            low = jnp.where(place[LOW_BIT] == z, 1, 0)
            for y in range(2):
                c_send[0, low, y, 0] = rows(z, place[Y_ORDER + 2 + y], 0, MAIN, FIRST)

    @pl.when(step == 1)
    def _():
        for z in range(2):
            low = jnp.where(place[LOW_BIT] == z, 1, 0)
            for y in range(2):
                c_keep[0, low, y, 0] = rows(z, place[Y_ORDER + 2 + y], 0, MAIN, FIRST)


def products(place, acts, cot, earlier):
    tokens = acts.shape[0]
    late = earlier is not None
    first = 2 if late else 0
    part = (2, 2, 2, 2, MAIN, HALF)
    piece = jax.ShapeDtypeStruct(part, jnp.float32)
    block = (1, 2, 2, 1, MAIN, HALF)
    by_x = pl.BlockSpec(block, lambda i, j, o: (i, 0, 0, o[HIGH_BIT] ^ j ^ 1, 0, 0))
    by_y = pl.BlockSpec(
        (2, 2, 1, 1, MAIN, HALF), lambda i, j, o: (0, 0, i, o[HIGH_BIT] ^ j ^ 1, 0, 0)
    )
    slot = 1 if late else 0
    at_first = pl.BlockSpec(
        block,
        lambda i, j, o: (slot, 0, 0, jnp.where(i == 0, o[HIGH_BIT] ^ j ^ 1, o[HIGH_BIT]), 0, 0),
    )
    at_second = pl.BlockSpec(
        block,
        lambda i, j, o: (slot, 0, 0, jnp.where(i == 0, o[HIGH_BIT] ^ 1, o[HIGH_BIT] ^ j ^ 1), 0, 0),
    )
    side_shape = jax.ShapeDtypeStruct((2, 2, 4, 4, SIDE, 2 * HALF), jnp.float32)
    side = pl.BlockSpec(
        (2, 1, 1, 4, SIDE, 2 * HALF),
        lambda i, j, o: (0, o[HIGH_BIT] ^ j ^ 1, first + i, 0, 0, 0),
    )
    any_spec = pl.BlockSpec(memory_space=pl.ANY)
    return pl.pallas_call(
        late_kernel if late else early_kernel,
        out_shape=[piece] * 5 + [side_shape],
        grid_spec=pltpu.PrefetchScalarGridSpec(
            num_scalar_prefetch=1,
            grid=(2, 2),
            in_specs=[
                pl.BlockSpec((tokens, 512), lambda i, j, o: (0, o[X_ORDER + first + i] * 2 + j)),
                pl.BlockSpec((tokens, 2 * HALF), lambda i, j, o: (0, 0)),
            ]
            + [any_spec] * (3 if late else 0),
            out_specs=[by_x, at_first, at_second, by_y, by_y, side],
            scratch_shapes=[pltpu.VMEM((512, 2 * HALF), jnp.float32)],
        ),
        input_output_aliases={3: 1, 4: 2, 5: 5} if late else {},
        compiler_params=pltpu.CompilerParams(vmem_limit_bytes=60 * 2**20),
        cost_estimate=pl.CostEstimate(
            flops=2 * tokens * 2048 * 1024 * (1 if late else 1),
            bytes_accessed=2 * tokens * 3072 + 4 * 2048 * 1024,
            transcendentals=0,
        ),
        name="products_late" if late else "products_early",
    )(place, acts, cot, *(earlier or ()))


def finish_kernel(
    here, total, total_other, weights, momentum, writers, own_new, own_mom, written, packed
):
    core, group = here[0], here[1]
    half, cols = total.shape

    def part(begin, rows):
        span = pl.ds(pl.multiple_of(begin, half), half)
        outer = weights[span, :]
        pseudo = outer - rows / 4
        mom = MOMENTUM * momentum[span, :] + pseudo
        packed[span, :cols] = outer - OUTER_RATE * (pseudo + MOMENTUM * mom)
        packed[span, cols:] = mom

    part(core * half, total[...])
    part((1 - core) * half, total_other[...])
    share = pl.ds(pl.multiple_of(group * 16, 16), 16)
    own_new[0] = packed[share, :cols]
    own_mom[0] = packed[share, cols:]
    count = writers.shape[1]
    by_column = jnp.broadcast_to(writers[...].astype(jnp.float32), (count, count))
    before = lax.broadcasted_iota(jnp.int32, (count, count), 0)
    row = lax.broadcasted_iota(jnp.int32, (count, count), 1)
    same = (by_column == by_column.T) & (before < row) & (before >> 4 == row >> 4)
    rank = jnp.sum(same.astype(jnp.int32), axis=0, keepdims=True)
    target = jnp.where(writers[...] == group, (row[:1] >> 4) * 8 + rank, -1)
    slots = lax.broadcasted_iota(jnp.int32, (written.shape[1], count), 0)
    placing = (target == slots).astype(jnp.float32)
    written[0] = jnp.dot(
        placing, packed[...], precision=lax.Precision.HIGHEST, preferred_element_type=jnp.float32
    )


def finish(here, total, total_other, weights, momentum, writers):
    cols = weights.shape[1]
    vmem = pl.BlockSpec(memory_space=pltpu.VMEM)
    return pl.pallas_call(
        finish_kernel,
        out_shape=[
            jax.ShapeDtypeStruct((1, 16, cols), jnp.float32),
            jax.ShapeDtypeStruct((1, 16, cols), jnp.float32),
            jax.ShapeDtypeStruct((1, 32, 2 * cols), jnp.float32),
        ],
        in_specs=[pl.BlockSpec(memory_space=pltpu.SMEM)] + [vmem] * 5,
        out_specs=[vmem] * 3,
        scratch_shapes=[pltpu.VMEM((64, 2 * cols), jnp.float32)],
        compiler_params=pltpu.CompilerParams(vmem_limit_bytes=16 * 2**20),
        name="finish",
    )(here, total, total_other, weights, momentum, writers)


def body(
    acts,
    cotangent,
    inner_weights,
    first_moment,
    second_moment,
    outer_weights,
    outer_momentum,
    writer_of,
):
    tokens = acts[0]
    upstream = cotangent[0]
    core = lax.axis_index("core")
    spot = {axis: lax.axis_index(axis) for axis in FSDP}

    flip = core == 1
    place = jnp.stack(
        ring_order(spot["x"], flip)
        + ring_order(spot["y"], flip)
        + ring_order(spot["y"], ~flip)
        + [spot["z"] & 1, spot["z"] >> 1]
    ).astype(jnp.int32)
    a_send, c_send, c_keep, b_send, b_keep, side = products(place, tokens, upstream, None)
    a_keep, c_send, c_keep, d_send, d_keep, side = products(
        place, tokens, upstream, (c_send, c_keep, side)
    )

    def along(axis, variant):
        return lambda value, step: ring_permute(value, axis, variant, step)

    last = []

    def turn(arrived, make):
        if last:
            arrived = behind(arrived, last[-1])
        last.append(make(arrived))
        return last[-1]

    x_one, y_one, x_two, y_two = along("x", 0), along("y", 0), along("x", 1), along("y", 1)
    a_got = x_one(a_send, 0)
    b_got = y_one(b_send, 0)
    c_got = x_two(c_send, 0)
    d_got = y_two(d_send, 0)
    s_got = line_permute(turn(side, lambda s: s[0]), 0)
    a_more = x_one(turn(a_got, lambda g: a_keep[0] + g[0]), 1)
    b_more = y_one(turn(b_got, lambda g: b_keep[0] + g[0]), 1)
    c_more = x_two(turn(c_got, lambda g: c_keep[0] + g[0]), 1)
    d_more = y_two(turn(d_got, lambda g: d_keep[0] + g[0]), 1)
    s_more = line_permute(turn(s_got, lambda g: side[1, 0] + g[0]), 1)
    a_in = y_one(turn(a_more, lambda g: (a_keep[1] + a_got[1] + g)[0]), 0)
    b_in = x_one(turn(b_more, lambda g: (b_keep[1] + b_got[1] + g)[0]), 0)
    a_in_own = y_one(turn(a_more, lambda g: (a_keep[1] + a_got[1] + g)[1]), 0)
    b_in_own = x_one(turn(b_more, lambda g: (b_keep[1] + b_got[1] + g)[1]), 0)
    a_last = y_one(turn((a_in, c_more), lambda g: c_keep[1, 0, 0] + c_got[1, 0, 0] + g[1][0, 0] + g[0][0]), 1)
    b_last = x_one(turn((b_in, d_more), lambda g: d_keep[1, 0, 0] + d_got[1, 0, 0] + g[1][0, 0] + g[0][0]), 1)
    c_sum = c_keep[1, :, 1] + c_got[1, :, 1] + c_more[:, 1]
    d_sum = d_keep[1, :, 1] + d_got[1, :, 1] + d_more[:, 1]
    x_got = x_one(turn((s_got, s_more), lambda g: side[1, 1, :2] + g[0][1, :2] + g[1][:2]), 0)
    z_got = line_permute(
        turn(
            (a_last, b_last),
            lambda g: jnp.concatenate([c_sum[0] + a_in[1] + g[0], d_sum[0] + b_in[1] + g[1]], axis=-1),
        ),
        0,
    )
    a_last_own = y_one(
        turn(a_in_own, lambda g: c_keep[1, 1, 0] + c_got[1, 1, 0] + c_more[1, 0] + g[0]), 1
    )
    b_last_own = x_one(
        turn(b_in_own, lambda g: d_keep[1, 1, 0] + d_got[1, 1, 0] + d_more[1, 0] + g[0]), 1
    )
    side_x = side[1, 1, 2:] + s_got[1, 2:] + s_more[2:]
    x_more = x_one(turn(x_got, lambda g: side_x[0] + g[0]), 1)
    own = jnp.concatenate(
        [c_sum[1] + a_in_own[1] + a_last_own, d_sum[1] + b_in_own[1] + b_last_own], axis=-1
    )
    z_more = line_permute(turn(z_got, lambda g: own[0] + g[0]), 1)
    side_y = side_x[1] + x_got[1]
    y_got = y_one(turn(x_more, lambda g: side_y[:2] + g[:2]), 0)
    side_z = side_y[2:] + x_more[2:]
    y_more = y_one(turn(y_got, lambda g: side_z[0] + g[0]), 1)
    side = side_z[1] + y_got[1] + y_more
    main_rows = own[1] + z_got[1] + z_more
    gradient = jnp.concatenate([main_rows, side], axis=0)
    stepped = adam_update(inner_weights[0], first_moment[0], second_moment[0], gradient)

    swap = [(0, 1), (1, 0)]
    halves = stepped.reshape(2, 32, stepped.shape[1])
    mine = lax.dynamic_index_in_dim(halves, core, 0, keepdims=False)
    other = lax.dynamic_index_in_dim(halves, 1 - core, 0, keepdims=False)
    pair = mine + lax.ppermute(other, "core", swap)
    total = pair + lax.ppermute(pair, "zh", swap)
    total_other = lax.ppermute(total, "core", swap)
    here = jnp.stack([core, lax.axis_index(GRP)]).astype(jnp.int32)
    return finish(here, total, total_other, outer_weights, outer_momentum, writer_of)


def solution(mesh):
    fine = Mesh(mesh.devices.reshape(2, 2, 4, 4, 4), GRP + FSDP)
    return jax.shard_map(
        body,
        mesh=fine,
        in_specs=(
            P(GRP, FSDP, None),
            P(GRP, FSDP, None),
            P(GRP, FSDP, None),
            P(GRP, FSDP, None),
            P(GRP, FSDP, None),
            P(FSDP, None),
            P(FSDP, None),
            P(FSDP, None),
        ),
        out_specs=(P(FSDP, GRP, None), P(FSDP, GRP, None), P(FSDP, GRP, None)),
        check_vma=False,
    )
```

```python
import functools

import jax
import jax.numpy as jnp
from jax import lax
from jax.experimental import pallas as pl
from jax.experimental.pallas import tpu as pltpu
from jax.sharding import Mesh, PartitionSpec as P

INNER_STEP = 100
BETA_ONE = 0.9
BETA_TWO = 0.95
INNER_RATE = 0.4
DECAY_RATE = 0.1
EPSILON = 1e-08
OUTER_RATE = 0.8
MOMENTUM = 0.9

GRP = ("zh", "core")
FSDP = ("x", "z", "y")
SIDE = 8
MAIN = 64 - SIDE
HALF = 512


def adam_update(weights, first_mom, second, gradient):
    first_new = BETA_ONE * first_mom + (1.0 - BETA_ONE) * gradient
    second_new = BETA_TWO * second + (1.0 - BETA_TWO) * gradient * gradient
    first_hat = first_new / (1.0 - BETA_ONE**INNER_STEP)
    second_hat = second_new / (1.0 - BETA_TWO**INNER_STEP)
    return weights - INNER_RATE * (
        first_hat / (jnp.sqrt(second_hat) + EPSILON) + DECAY_RATE * weights
    )


def ring_partners(p, flip):
    near, far = p ^ 1, 3 - p
    return (far, near) if flip else (near, far)


def ring_block(p, flip, rank):
    return p ^ (2, 1 + 2 * flip, 3 - 2 * flip, 0)[rank]


def ring_permute(value, axis, variant, step):
    perm = []
    for core in range(2):
        for p in range(4):
            q = ring_partners(p, (core + variant) % 2)[step]
            perm.append((core * 4 + p, core * 4 + q))
    return lax.ppermute(value, ("core", axis), perm)


def line_permute(value, step):
    bit = 1 + step
    return lax.ppermute(value, "z", [(p, p ^ bit) for p in range(4)])


def behind(value, earlier):
    return lax.optimization_barrier((value, earlier))[0]


CORE, X, Y, Z = range(4)


def y_block(place, variant, rank):
    return ring_block(place[Y], place[CORE] ^ variant, rank)


def z_low(place):
    return place[Z] & 1


def z_high(place):
    return place[Z] >> 1


def product_rows(acts, cot, result):
    result[...] = lax.dot_general(
        acts[...], cot[...], (((0,), (0,)), ((), ())), preferred_element_type=jnp.float32
    )

    def rows(z, y, start, count, cols):
        offset = pl.multiple_of(z * 256 + y * 64 + start, 8)
        return result[pl.ds(offset, count), cols]

    return rows


FIRST, SECOND = slice(0, HALF), slice(HALF, 2 * HALF)


def sides(place, side, rows):
    for z in range(2):
        low = jnp.where(z_low(place) == z, 1, 0)
        for y in range(4):
            side[low, 0, 0, y] = rows(z, y_block(place, 0, y), MAIN, SIDE, slice(0, 2 * HALF))


def early_kernel(place, acts, cot, a_send, c_send, c_keep, b_send, b_keep, side, result):
    rows = product_rows(acts, cot, result)
    sides(place, side, rows)
    step = pl.program_id(0)
    for z in range(2):
        low = jnp.where(z_low(place) == z, 1, 0)
        for y in range(2):
            a_send[0, low, y, 0] = rows(z, y_block(place, 1, y), 0, MAIN, FIRST)
            b_send[y, low, 0, 0] = rows(z, y_block(place, 0, y), 0, MAIN, SECOND)
            b_keep[y, low, 0, 0] = rows(z, y_block(place, 0, 2 + y), 0, MAIN, SECOND)

    @pl.when(step == 0)
    def _():
        for z in range(2):
            low = jnp.where(z_low(place) == z, 1, 0)
            for y in range(2):
                c_send[0, low, y, 0] = rows(z, y_block(place, 1, 2 + y), 0, MAIN, FIRST)

    @pl.when(step == 1)
    def _():
        for z in range(2):
            low = jnp.where(z_low(place) == z, 1, 0)
            for y in range(2):
                c_keep[0, low, y, 0] = rows(z, y_block(place, 1, 2 + y), 0, MAIN, FIRST)


def late_kernel(
    place, acts, cot, c_send_in, c_keep_in, side_in, a_keep, c_send, c_keep, b_send, b_keep, side, result
):
    rows = product_rows(acts, cot, result)
    sides(place, side, rows)
    step = pl.program_id(0)
    for z in range(2):
        low = jnp.where(z_low(place) == z, 1, 0)
        for y in range(2):
            a_keep[0, low, y, 0] = rows(z, y_block(place, 1, y), 0, MAIN, FIRST)
            b_send[y, low, 0, 0] = rows(z, y_block(place, 1, y), 0, MAIN, SECOND)
            b_keep[y, low, 0, 0] = rows(z, y_block(place, 1, 2 + y), 0, MAIN, SECOND)

    @pl.when(step == 0)
    def _():
        for z in range(2):
            low = jnp.where(z_low(place) == z, 1, 0)
            for y in range(2):
                c_send[0, low, y, 0] = rows(z, y_block(place, 1, 2 + y), 0, MAIN, FIRST)

    @pl.when(step == 1)
    def _():
        for z in range(2):
            low = jnp.where(z_low(place) == z, 1, 0)
            for y in range(2):
                c_keep[0, low, y, 0] = rows(z, y_block(place, 1, 2 + y), 0, MAIN, FIRST)


def products(place, acts, cot, earlier):
    tokens = acts.shape[0]
    late = earlier is not None
    first = 2 if late else 0
    part = (2, 2, 2, 2, MAIN, HALF)
    piece = jax.ShapeDtypeStruct(part, jnp.float32)
    block = (1, 2, 2, 1, MAIN, HALF)
    by_x = pl.BlockSpec(block, lambda i, j, o: (i, 0, 0, z_high(o) ^ j ^ 1, 0, 0))
    by_y = pl.BlockSpec(
        (2, 2, 1, 1, MAIN, HALF), lambda i, j, o: (0, 0, i, z_high(o) ^ j ^ 1, 0, 0)
    )
    slot = 1 if late else 0
    at_first = pl.BlockSpec(
        block,
        lambda i, j, o: (slot, 0, 0, jnp.where(i == 0, z_high(o) ^ j ^ 1, z_high(o)), 0, 0),
    )
    at_second = pl.BlockSpec(
        block,
        lambda i, j, o: (slot, 0, 0, jnp.where(i == 0, z_high(o) ^ 1, z_high(o) ^ j ^ 1), 0, 0),
    )
    side_shape = jax.ShapeDtypeStruct((2, 2, 4, 4, SIDE, 2 * HALF), jnp.float32)
    side = pl.BlockSpec(
        (2, 1, 1, 4, SIDE, 2 * HALF),
        lambda i, j, o: (0, z_high(o) ^ j ^ 1, first + i, 0, 0, 0),
    )
    any_spec = pl.BlockSpec(memory_space=pl.ANY)

    def x_block(i, o):
        near, far = (ring_block(o[X], o[CORE], first + rank) for rank in range(2))
        return jnp.where(i == 0, near, far)

    return pl.pallas_call(
        late_kernel if late else early_kernel,
        out_shape=[piece] * 5 + [side_shape],
        grid_spec=pltpu.PrefetchScalarGridSpec(
            num_scalar_prefetch=1,
            grid=(2, 2),
            in_specs=[
                pl.BlockSpec((tokens, 512), lambda i, j, o: (0, x_block(i, o) * 2 + j)),
                pl.BlockSpec((tokens, 2 * HALF), lambda i, j, o: (0, 0)),
            ]
            + [any_spec] * (3 if late else 0),
            out_specs=[by_x, at_first, at_second, by_y, by_y, side],
            scratch_shapes=[pltpu.VMEM((512, 2 * HALF), jnp.float32)],
        ),
        input_output_aliases={3: 1, 4: 2, 5: 5} if late else {},
        compiler_params=pltpu.CompilerParams(vmem_limit_bytes=60 * 2**20),
        cost_estimate=pl.CostEstimate(
            flops=2 * tokens * 2048 * 1024 * (1 if late else 1),
            bytes_accessed=2 * tokens * 3072 + 4 * 2048 * 1024,
            transcendentals=0,
        ),
        name="products_late" if late else "products_early",
    )(place, acts, cot, *(earlier or ()))


def finish_kernel(
    here, total, total_other, weights, momentum, writers, own_new, own_mom, written, packed
):
    core, group = here[0], here[1]
    half, cols = total.shape

    def part(begin, rows):
        span = pl.ds(pl.multiple_of(begin, half), half)
        outer = weights[span, :]
        pseudo = outer - rows / 4
        mom = MOMENTUM * momentum[span, :] + pseudo
        packed[span, :cols] = outer - OUTER_RATE * (pseudo + MOMENTUM * mom)
        packed[span, cols:] = mom

    part(core * half, total[...])
    part((1 - core) * half, total_other[...])
    share = pl.ds(pl.multiple_of(group * 16, 16), 16)
    own_new[0] = packed[share, :cols]
    own_mom[0] = packed[share, cols:]
    count = writers.shape[1]
    by_column = jnp.broadcast_to(writers[...].astype(jnp.float32), (count, count))
    before = lax.broadcasted_iota(jnp.int32, (count, count), 0)
    row = lax.broadcasted_iota(jnp.int32, (count, count), 1)
    same = (by_column == by_column.T) & (before < row) & (before >> 4 == row >> 4)
    rank = jnp.sum(same.astype(jnp.int32), axis=0, keepdims=True)
    target = jnp.where(writers[...] == group, (row[:1] >> 4) * 8 + rank, -1)
    slots = lax.broadcasted_iota(jnp.int32, (written.shape[1], count), 0)
    placing = (target == slots).astype(jnp.float32)
    written[0] = jnp.dot(
        placing, packed[...], precision=lax.Precision.HIGHEST, preferred_element_type=jnp.float32
    )


def finish(here, total, total_other, weights, momentum, writers):
    cols = weights.shape[1]
    vmem = pl.BlockSpec(memory_space=pltpu.VMEM)
    return pl.pallas_call(
        finish_kernel,
        out_shape=[
            jax.ShapeDtypeStruct((1, 16, cols), jnp.float32),
            jax.ShapeDtypeStruct((1, 16, cols), jnp.float32),
            jax.ShapeDtypeStruct((1, 32, 2 * cols), jnp.float32),
        ],
        in_specs=[pl.BlockSpec(memory_space=pltpu.SMEM)] + [vmem] * 5,
        out_specs=[vmem] * 3,
        scratch_shapes=[pltpu.VMEM((64, 2 * cols), jnp.float32)],
        compiler_params=pltpu.CompilerParams(vmem_limit_bytes=16 * 2**20),
        name="finish",
    )(here, total, total_other, weights, momentum, writers)


def body(
    acts,
    cotangent,
    inner_weights,
    first_moment,
    second_moment,
    outer_weights,
    outer_momentum,
    writer_of,
):
    tokens = acts[0]
    upstream = cotangent[0]
    core = lax.axis_index("core")

    place = jnp.stack([core] + [lax.axis_index(axis) for axis in ("x", "y", "z")]).astype(jnp.int32)
    a_send, c_send, c_keep, b_send, b_keep, side = products(place, tokens, upstream, None)
    a_keep, c_send, c_keep, d_send, d_keep, side = products(
        place, tokens, upstream, (c_send, c_keep, side)
    )

    def along(axis, variant):
        return lambda value, step: ring_permute(value, axis, variant, step)

    last = []

    def turn(arrived, make):
        if last:
            arrived = behind(arrived, last[-1])
        last.append(make(arrived))
        return last[-1]

    x_one, y_one, x_two, y_two = along("x", 0), along("y", 0), along("x", 1), along("y", 1)
    a_got = x_one(a_send, 0)
    b_got = y_one(b_send, 0)
    c_got = x_two(c_send, 0)
    d_got = y_two(d_send, 0)
    s_got = line_permute(turn(side, lambda s: s[0]), 0)
    a_more = x_one(turn(a_got, lambda g: a_keep[0] + g[0]), 1)
    b_more = y_one(turn(b_got, lambda g: b_keep[0] + g[0]), 1)
    c_more = x_two(turn(c_got, lambda g: c_keep[0] + g[0]), 1)
    d_more = y_two(turn(d_got, lambda g: d_keep[0] + g[0]), 1)
    s_more = line_permute(turn(s_got, lambda g: side[1, 0] + g[0]), 1)
    a_in = y_two(turn(a_more, lambda g: (a_keep[1] + a_got[1] + g)[0]), 0)
    b_in = x_one(turn(b_more, lambda g: (b_keep[1] + b_got[1] + g)[0]), 0)
    a_in_own = y_two(turn(a_more, lambda g: (a_keep[1] + a_got[1] + g)[1]), 0)
    b_in_own = x_one(turn(b_more, lambda g: (b_keep[1] + b_got[1] + g)[1]), 0)
    a_last = y_two(turn((a_in, c_more), lambda g: c_keep[1, 0, 0] + c_got[1, 0, 0] + g[1][0, 0] + g[0][0]), 1)
    b_last = x_one(turn((b_in, d_more), lambda g: d_keep[1, 0, 0] + d_got[1, 0, 0] + g[1][0, 0] + g[0][0]), 1)
    c_sum = c_keep[1, :, 1] + c_got[1, :, 1] + c_more[:, 1]
    d_sum = d_keep[1, :, 1] + d_got[1, :, 1] + d_more[:, 1]
    x_got = x_one(turn((s_got, s_more), lambda g: side[1, 1, :2] + g[0][1, :2] + g[1][:2]), 0)
    z_got = line_permute(
        turn(
            (a_last, b_last),
            lambda g: jnp.concatenate([c_sum[0] + a_in[1] + g[0], d_sum[0] + b_in[1] + g[1]], axis=-1),
        ),
        0,
    )
    a_last_own = y_two(
        turn(a_in_own, lambda g: c_keep[1, 1, 0] + c_got[1, 1, 0] + c_more[1, 0] + g[0]), 1
    )
    b_last_own = x_one(
        turn(b_in_own, lambda g: d_keep[1, 1, 0] + d_got[1, 1, 0] + d_more[1, 0] + g[0]), 1
    )
    side_x = side[1, 1, 2:] + s_got[1, 2:] + s_more[2:]
    x_more = x_one(turn(x_got, lambda g: side_x[0] + g[0]), 1)
    own = jnp.concatenate(
        [c_sum[1] + a_in_own[1] + a_last_own, d_sum[1] + b_in_own[1] + b_last_own], axis=-1
    )
    z_more = line_permute(turn(z_got, lambda g: own[0] + g[0]), 1)
    side_y = side_x[1] + x_got[1]
    y_got = y_one(turn(x_more, lambda g: side_y[:2] + g[:2]), 0)
    side_z = side_y[2:] + x_more[2:]
    y_more = y_one(turn(y_got, lambda g: side_z[0] + g[0]), 1)
    side = side_z[1] + y_got[1] + y_more
    main_rows = own[1] + z_got[1] + z_more
    gradient = jnp.concatenate([main_rows, side], axis=0)
    stepped = adam_update(inner_weights[0], first_moment[0], second_moment[0], gradient)

    swap = [(0, 1), (1, 0)]
    halves = stepped.reshape(2, 32, stepped.shape[1])
    mine = lax.dynamic_index_in_dim(halves, core, 0, keepdims=False)
    other = lax.dynamic_index_in_dim(halves, 1 - core, 0, keepdims=False)
    pair = mine + lax.ppermute(other, "core", swap)
    total = pair + lax.ppermute(pair, "zh", swap)
    total_other = lax.ppermute(total, "core", swap)
    here = jnp.stack([core, lax.axis_index(GRP)]).astype(jnp.int32)
    return finish(here, total, total_other, outer_weights, outer_momentum, writer_of)


def solution(mesh):
    fine = Mesh(mesh.devices.reshape(2, 2, 4, 4, 4), GRP + FSDP)
    return jax.shard_map(
        body,
        mesh=fine,
        in_specs=(
            P(GRP, FSDP, None),
            P(GRP, FSDP, None),
            P(GRP, FSDP, None),
            P(GRP, FSDP, None),
            P(GRP, FSDP, None),
            P(FSDP, None),
            P(FSDP, None),
            P(FSDP, None),
        ),
        out_specs=(P(FSDP, GRP, None), P(FSDP, GRP, None), P(FSDP, GRP, None)),
        check_vma=False,
    )
```

```python
import functools

import jax
import jax.numpy as jnp
from jax import lax
from jax.experimental import pallas as pl
from jax.experimental.pallas import tpu as pltpu
from jax.sharding import Mesh, PartitionSpec as P

INNER_STEP = 100
BETA_ONE = 0.9
BETA_TWO = 0.95
INNER_RATE = 0.4
DECAY_RATE = 0.1
EPSILON = 1e-08
OUTER_RATE = 0.8
MOMENTUM = 0.9

GRP = ("zh", "core")
FSDP = ("x", "z", "y")
SIDE = 8
MAIN = 64 - SIDE
HALF = 512


def adam_update(weights, first_mom, second, gradient):
    first_new = BETA_ONE * first_mom + (1.0 - BETA_ONE) * gradient
    second_new = BETA_TWO * second + (1.0 - BETA_TWO) * gradient * gradient
    first_hat = first_new / (1.0 - BETA_ONE**INNER_STEP)
    second_hat = second_new / (1.0 - BETA_TWO**INNER_STEP)
    return weights - INNER_RATE * (
        first_hat / (jnp.sqrt(second_hat) + EPSILON) + DECAY_RATE * weights
    )


def ring_partners(p, flip):
    near, far = p ^ 1, 3 - p
    return (far, near) if flip else (near, far)


def ring_block(p, flip, rank):
    return p ^ (2, 1 + 2 * flip, 3 - 2 * flip, 0)[rank]


def ring_permute(value, axis, variant, step):
    perm = []
    for core in range(2):
        for p in range(4):
            q = ring_partners(p, (core + variant) % 2)[step]
            perm.append((core * 4 + p, core * 4 + q))
    return lax.ppermute(value, ("core", axis), perm)


def line_permute(value, step):
    bit = 1 + step
    return lax.ppermute(value, "z", [(p, p ^ bit) for p in range(4)])


def behind(value, earlier):
    return lax.optimization_barrier((value, earlier))[0]


CORE, X, Y, Z = range(4)


def y_block(place, variant, rank):
    return ring_block(place[Y], place[CORE] ^ variant, rank)


def z_low(place):
    return place[Z] & 1


def z_high(place):
    return place[Z] >> 1


def product_rows(acts, cot, result):
    result[...] = lax.dot_general(
        acts[...], cot[...], (((0,), (0,)), ((), ())), preferred_element_type=jnp.float32
    )

    def rows(z, y, start, count, cols):
        offset = pl.multiple_of(z * 256 + y * 64 + start, 8)
        return result[pl.ds(offset, count), cols]

    return rows


FIRST, SECOND = slice(0, HALF), slice(HALF, 2 * HALF)


def sides(place, side, rows):
    for z in range(2):
        low = jnp.where(z_low(place) == z, 1, 0)
        for y in range(4):
            side[low, 0, 0, y] = rows(z, y_block(place, 0, y), MAIN, SIDE, slice(0, 2 * HALF))


def early_kernel(place, acts, cot, a_send, c_send, c_keep, b_send, b_keep, side, result):
    rows = product_rows(acts, cot, result)
    sides(place, side, rows)
    step = pl.program_id(0)
    for z in range(2):
        low = jnp.where(z_low(place) == z, 1, 0)
        for y in range(2):
            a_send[0, low, y, 0] = rows(z, y_block(place, 1, y), 0, MAIN, FIRST)
            b_send[y, low, 0, 0] = rows(z, y_block(place, 0, y), 0, MAIN, SECOND)
            b_keep[y, low, 0, 0] = rows(z, y_block(place, 0, 2 + y), 0, MAIN, SECOND)

    @pl.when(step == 0)
    def _():
        for z in range(2):
            low = jnp.where(z_low(place) == z, 1, 0)
            for y in range(2):
                c_send[0, low, y, 0] = rows(z, y_block(place, 1, 2 + y), 0, MAIN, FIRST)

    @pl.when(step == 1)
    def _():
        for z in range(2):
            low = jnp.where(z_low(place) == z, 1, 0)
            for y in range(2):
                c_keep[0, low, y, 0] = rows(z, y_block(place, 1, 2 + y), 0, MAIN, FIRST)


def late_kernel(
    place, acts, cot, c_send_in, c_keep_in, side_in, a_keep, c_send, c_keep, b_send, b_keep, side, result
):
    rows = product_rows(acts, cot, result)
    sides(place, side, rows)
    step = pl.program_id(0)
    for z in range(2):
        low = jnp.where(z_low(place) == z, 1, 0)
        for y in range(2):
            a_keep[0, low, y, 0] = rows(z, y_block(place, 1, y), 0, MAIN, FIRST)
            b_send[y, low, 0, 0] = rows(z, y_block(place, 1, y), 0, MAIN, SECOND)
            b_keep[y, low, 0, 0] = rows(z, y_block(place, 1, 2 + y), 0, MAIN, SECOND)

    @pl.when(step == 0)
    def _():
        for z in range(2):
            low = jnp.where(z_low(place) == z, 1, 0)
            for y in range(2):
                c_send[0, low, y, 0] = rows(z, y_block(place, 1, 2 + y), 0, MAIN, FIRST)

    @pl.when(step == 1)
    def _():
        for z in range(2):
            low = jnp.where(z_low(place) == z, 1, 0)
            for y in range(2):
                c_keep[0, low, y, 0] = rows(z, y_block(place, 1, 2 + y), 0, MAIN, FIRST)


def products(place, acts, cot, earlier):
    tokens = acts.shape[0]
    late = earlier is not None
    first = 2 if late else 0
    part = (2, 2, 2, 2, MAIN, HALF)
    piece = jax.ShapeDtypeStruct(part, jnp.float32)
    block = (1, 2, 2, 1, MAIN, HALF)
    by_x = pl.BlockSpec(block, lambda i, j, o: (i, 0, 0, z_high(o) ^ j ^ 1, 0, 0))
    by_y = pl.BlockSpec(
        (2, 2, 1, 1, MAIN, HALF), lambda i, j, o: (0, 0, i, z_high(o) ^ j ^ 1, 0, 0)
    )
    slot = 1 if late else 0
    at_first = pl.BlockSpec(
        block,
        lambda i, j, o: (slot, 0, 0, jnp.where(i == 0, z_high(o) ^ j ^ 1, z_high(o)), 0, 0),
    )
    at_second = pl.BlockSpec(
        block,
        lambda i, j, o: (slot, 0, 0, jnp.where(i == 0, z_high(o) ^ 1, z_high(o) ^ j ^ 1), 0, 0),
    )
    side_shape = jax.ShapeDtypeStruct((2, 2, 4, 4, SIDE, 2 * HALF), jnp.float32)
    side = pl.BlockSpec(
        (2, 1, 1, 4, SIDE, 2 * HALF),
        lambda i, j, o: (0, z_high(o) ^ j ^ 1, first + i, 0, 0, 0),
    )
    any_spec = pl.BlockSpec(memory_space=pl.ANY)

    def x_block(i, o):
        near, far = (ring_block(o[X], o[CORE], first + rank) for rank in range(2))
        return jnp.where(i == 0, near, far)

    return pl.pallas_call(
        late_kernel if late else early_kernel,
        out_shape=[piece] * 5 + [side_shape],
        grid_spec=pltpu.PrefetchScalarGridSpec(
            num_scalar_prefetch=1,
            grid=(2, 2),
            in_specs=[
                pl.BlockSpec((tokens, 512), lambda i, j, o: (0, x_block(i, o) * 2 + j)),
                pl.BlockSpec((tokens, 2 * HALF), lambda i, j, o: (0, 0)),
            ]
            + [any_spec] * (3 if late else 0),
            out_specs=[by_x, at_first, at_second, by_y, by_y, side],
            scratch_shapes=[pltpu.VMEM((512, 2 * HALF), jnp.float32)],
        ),
        input_output_aliases={3: 1, 4: 2, 5: 5} if late else {},
        compiler_params=pltpu.CompilerParams(vmem_limit_bytes=60 * 2**20),
        cost_estimate=pl.CostEstimate(
            flops=2 * tokens * 2048 * 1024 * (1 if late else 1),
            bytes_accessed=2 * tokens * 3072 + 4 * 2048 * 1024,
            transcendentals=0,
        ),
        name="products_late" if late else "products_early",
    )(place, acts, cot, *(earlier or ()))


def finish_kernel(
    here, total, total_other, weights, momentum, writers, own_new, own_mom, written, packed
):
    core, group = here[0], here[1]
    half, cols = total.shape

    def part(begin, rows):
        span = pl.ds(pl.multiple_of(begin, half), half)
        outer = weights[span, :]
        pseudo = outer - rows / 4
        mom = MOMENTUM * momentum[span, :] + pseudo
        packed[span, :cols] = outer - OUTER_RATE * (pseudo + MOMENTUM * mom)
        packed[span, cols:] = mom

    part(core * half, total[...])
    part((1 - core) * half, total_other[...])
    share = pl.ds(pl.multiple_of(group * 16, 16), 16)
    own_new[0] = packed[share, :cols]
    own_mom[0] = packed[share, cols:]
    count = writers.shape[1]
    by_column = jnp.broadcast_to(writers[...].astype(jnp.float32), (count, count))
    before = lax.broadcasted_iota(jnp.int32, (count, count), 0)
    row = lax.broadcasted_iota(jnp.int32, (count, count), 1)
    same = (by_column == by_column.T) & (before < row) & (before >> 4 == row >> 4)
    rank = jnp.sum(same.astype(jnp.int32), axis=0, keepdims=True)
    target = jnp.where(writers[...] == group, (row[:1] >> 4) * 8 + rank, -1)
    slots = lax.broadcasted_iota(jnp.int32, (written.shape[1], count), 0)
    placing = (target == slots).astype(jnp.float32)
    written[0] = jnp.dot(
        placing, packed[...], precision=lax.Precision.HIGHEST, preferred_element_type=jnp.float32
    )


def finish(here, total, total_other, weights, momentum, writers):
    cols = weights.shape[1]
    vmem = pl.BlockSpec(memory_space=pltpu.VMEM)
    return pl.pallas_call(
        finish_kernel,
        out_shape=[
            jax.ShapeDtypeStruct((1, 16, cols), jnp.float32),
            jax.ShapeDtypeStruct((1, 16, cols), jnp.float32),
            jax.ShapeDtypeStruct((1, 32, 2 * cols), jnp.float32),
        ],
        in_specs=[pl.BlockSpec(memory_space=pltpu.SMEM)] + [vmem] * 5,
        out_specs=[vmem] * 3,
        scratch_shapes=[pltpu.VMEM((64, 2 * cols), jnp.float32)],
        compiler_params=pltpu.CompilerParams(vmem_limit_bytes=16 * 2**20),
        name="finish",
    )(here, total, total_other, weights, momentum, writers)


def body(
    acts,
    cotangent,
    inner_weights,
    first_moment,
    second_moment,
    outer_weights,
    outer_momentum,
    writer_of,
):
    tokens = acts[0]
    upstream = cotangent[0]
    core = lax.axis_index("core")

    place = jnp.stack([core] + [lax.axis_index(axis) for axis in ("x", "y", "z")]).astype(jnp.int32)
    a_send, c_send, c_keep, b_send, b_keep, side = products(place, tokens, upstream, None)
    a_keep, c_send, c_keep, d_send, d_keep, side = products(
        place, tokens, upstream, (c_send, c_keep, side)
    )

    def along(axis, variant):
        return lambda value, step: ring_permute(value, axis, variant, step)

    last = []

    def turn(arrived, make):
        if last:
            arrived = behind(arrived, last[-1])
        last.append(make(arrived))
        return last[-1]

    x_one, y_one, x_two, y_two = along("x", 0), along("y", 0), along("x", 1), along("y", 1)
    a_got = x_one(a_send, 0)
    b_got = y_one(b_send, 0)
    c_got = x_two(c_send, 0)
    d_got = y_two(d_send, 0)
    s_got = line_permute(turn(side, lambda s: s[0]), 0)
    a_more = x_one(turn(a_got, lambda g: a_keep[0] + g[0]), 1)
    b_more = y_one(turn(b_got, lambda g: b_keep[0] + g[0]), 1)
    c_more = x_two(turn(c_got, lambda g: c_keep[0] + g[0]), 1)
    d_more = y_two(turn(d_got, lambda g: d_keep[0] + g[0]), 1)
    s_more = line_permute(turn(s_got, lambda g: side[1, 0] + g[0]), 1)
    a_in = y_two(turn(a_more, lambda g: (a_keep[1] + a_got[1] + g)[0]), 0)
    b_in = x_one(turn(b_more, lambda g: (b_keep[1] + b_got[1] + g)[0]), 0)
    a_last = y_two(turn((a_in, c_more), lambda g: c_keep[1, 0, 0] + c_got[1, 0, 0] + g[1][0, 0] + g[0][0]), 1)
    b_last = x_one(turn((b_in, d_more), lambda g: d_keep[1, 0, 0] + d_got[1, 0, 0] + g[1][0, 0] + g[0][0]), 1)
    c_sum = c_keep[1, :, 1] + c_got[1, :, 1] + c_more[:, 1]
    d_sum = d_keep[1, :, 1] + d_got[1, :, 1] + d_more[:, 1]
    a_in_own = y_two(turn(a_more, lambda g: (a_keep[1] + a_got[1] + g)[1]), 0)
    b_in_own = x_one(turn(b_more, lambda g: (b_keep[1] + b_got[1] + g)[1]), 0)
    x_got = x_one(turn((s_got, s_more), lambda g: side[1, 1, :2] + g[0][1, :2] + g[1][:2]), 0)
    z_got = line_permute(
        turn(
            (a_last, b_last),
            lambda g: jnp.concatenate([c_sum[0] + a_in[1] + g[0], d_sum[0] + b_in[1] + g[1]], axis=-1),
        ),
        0,
    )
    a_last_own = y_two(
        turn(a_in_own, lambda g: c_keep[1, 1, 0] + c_got[1, 1, 0] + c_more[1, 0] + g[0]), 1
    )
    b_last_own = x_one(
        turn(b_in_own, lambda g: d_keep[1, 1, 0] + d_got[1, 1, 0] + d_more[1, 0] + g[0]), 1
    )
    side_x = side[1, 1, 2:] + s_got[1, 2:] + s_more[2:]
    x_more = x_one(turn(x_got, lambda g: side_x[0] + g[0]), 1)
    own = jnp.concatenate(
        [c_sum[1] + a_in_own[1] + a_last_own, d_sum[1] + b_in_own[1] + b_last_own], axis=-1
    )
    z_more = line_permute(turn(z_got, lambda g: own[0] + g[0]), 1)
    side_y = side_x[1] + x_got[1]
    y_got = y_one(turn(x_more, lambda g: side_y[:2] + g[:2]), 0)
    side_z = side_y[2:] + x_more[2:]
    y_more = y_one(turn(y_got, lambda g: side_z[0] + g[0]), 1)
    side = side_z[1] + y_got[1] + y_more
    main_rows = own[1] + z_got[1] + z_more
    gradient = jnp.concatenate([main_rows, side], axis=0)
    stepped = adam_update(inner_weights[0], first_moment[0], second_moment[0], gradient)

    swap = [(0, 1), (1, 0)]
    halves = stepped.reshape(2, 32, stepped.shape[1])
    mine = lax.dynamic_index_in_dim(halves, core, 0, keepdims=False)
    other = lax.dynamic_index_in_dim(halves, 1 - core, 0, keepdims=False)
    pair = mine + lax.ppermute(other, "core", swap)
    total = pair + lax.ppermute(pair, "zh", swap)
    total_other = lax.ppermute(total, "core", swap)
    here = jnp.stack([core, lax.axis_index(GRP)]).astype(jnp.int32)
    return finish(here, total, total_other, outer_weights, outer_momentum, writer_of)


def solution(mesh):
    fine = Mesh(mesh.devices.reshape(2, 2, 4, 4, 4), GRP + FSDP)
    return jax.shard_map(
        body,
        mesh=fine,
        in_specs=(
            P(GRP, FSDP, None),
            P(GRP, FSDP, None),
            P(GRP, FSDP, None),
            P(GRP, FSDP, None),
            P(GRP, FSDP, None),
            P(FSDP, None),
            P(FSDP, None),
            P(FSDP, None),
        ),
        out_specs=(P(FSDP, GRP, None), P(FSDP, GRP, None), P(FSDP, GRP, None)),
        check_vma=False,
    )
```
